32 devices in a mesh: depth: 8 (over z, y), lat: 4 (over x, core).
Axes of the slice: x: 2, y: 2, z: 4, core: 2. Of those that a mesh axis runs over, the one named last changes fastest.
Arguments:
- densities: float32 [4, 256, 64], P('lat', 'depth'), may hold values from -6 to 6
- source: float32 [4, 256, 64], P('lat', 'depth'), may hold values from -6 to 6
- jacobian: float32 [4, 256, 4096], P('lat', 'depth'), may hold values from -0.75 to 0.75
- pattern: int32 [8, 8], replicated, may hold values 0 or 1
- transport: float32 [4, 256, 64], P('lat', 'depth'), may hold values from 0.2 to 1
- lateral: float32 [4, 256, 64], P('lat', 'depth'), may hold values from 0.1 to 1
- neighbours: int32 [4, 4], P('lat'), may hold values from 0 to 3, as said below
- factor: float32 [4, 256, 4096], P('lat', 'depth'), may hold values from -0.0009765625 to 0.001953125
- coupling: float32 [4, 256, 64], P('lat', 'depth'), may hold values from 512 to 2048
Outputs:
- correction: float32 [4, 256, 64], P('lat', 'depth')
The draws below stay inside these ranges and needn't reach their ends.
Inputs may be any that keep to these rules, and one draw needn't show every extreme that they name: Each line's four neighbours (previous row, next row, previous place, next place) in a periodic arrangement of the lines in rows of 4, under a relabelling of the lines drawn from the seed.
All inputs are finite; a program needn't handle non-finite values.
Results may differ from the reference program's by a relative error of at most 0.0003.
Values sent between devices are 32-bit elements; how exact they have to be, the bound alone decides.
A program may use at most 128 MiB of HBM per device.

```python
import math
import jax
import jax.numpy as jnp
from jax import lax

SPECIES = 64
TILE = 8
NTILE = 8
LATERAL_LINES = 4
DEPTH_CELLS = 256
LINES_PER_ROW = 4


def factor_parts(key):
    base = jax.random.fold_in(key, 4101)
    random_keys = jax.random.split(base, 7)
    share = 0.5
    slow = jax.random.bernoulli(random_keys[0], share, (LATERAL_LINES, 1, SPECIES))
    fast_rate = jnp.exp(-1.0 / jax.random.uniform(random_keys[1], (LATERAL_LINES, 1, SPECIES), jnp.float32, 30.0, 50.0))
    slow_rate = jnp.exp(jnp.log(jax.random.uniform(random_keys[2], (LATERAL_LINES, 1, SPECIES), jnp.float32, 0.3, 0.6)) / DEPTH_CELLS)
    rate = jnp.where(slow, slow_rate, fast_rate)
    damaged_cells = jax.random.randint(random_keys[3], (3,), 0, DEPTH_CELLS)
    impacted_lines = jnp.zeros((DEPTH_CELLS,), jnp.float32).at[damaged_cells].set(1.0)
    losses = jax.random.uniform(random_keys[4], (LATERAL_LINES, 1, SPECIES), jnp.float32, 0.5, 0.8)
    hitting = jnp.logical_and(slow, impacted_lines[None, :, None] > 0.5)
    rate = rate * jnp.where(hitting, losses, 1.0)
    spread = 1.4 / math.sqrt(SPECIES * DEPTH_CELLS)
    mixing = jnp.clip(jax.random.normal(random_keys[5], (LATERAL_LINES, DEPTH_CELLS, SPECIES, SPECIES), jnp.float32), -6.0, 6.0) * spread
    identity = jnp.eye(SPECIES, dtype=jnp.float32)
    matrix = mixing * (1.0 - identity) + identity * rate[..., None]
    lowest = float(DEPTH_CELLS * DEPTH_CELLS // 128)
    highest = float(DEPTH_CELLS * DEPTH_CELLS // 32)
    coupling = jnp.exp(jax.random.uniform(random_keys[6], (LATERAL_LINES, DEPTH_CELLS, SPECIES), jnp.float32, math.log(lowest), math.log(highest)))
    inverse = matrix / coupling[:, :, None, :]
    return (inverse.reshape(LATERAL_LINES, DEPTH_CELLS, SPECIES * SPECIES), coupling)


def draw_factor(key, part):
    inverse, coupling = factor_parts(key)
    return inverse


def draw_coupling(key, part):
    inverse, coupling = factor_parts(key)
    return coupling


def draw_neighbours(key, part):
    line_labels = jax.random.permutation(jax.random.fold_in(key, 77), LATERAL_LINES).astype(jnp.int32)
    line_position = jnp.arange(LATERAL_LINES, dtype=jnp.int32)
    lateral_row_count = LATERAL_LINES // LINES_PER_ROW
    lateral_row_index = line_position // LINES_PER_ROW
    slot_index = line_position % LINES_PER_ROW

    def label_at(lateral_row_value, slot_value):
        return line_labels[lateral_row_value % lateral_row_count * LINES_PER_ROW + slot_value % LINES_PER_ROW]
    by_position = jnp.stack([label_at(lateral_row_index - 1, slot_index), label_at(lateral_row_index + 1, slot_index), label_at(lateral_row_index, slot_index - 1), label_at(lateral_row_index, slot_index + 1)], axis=1)
    table = jnp.zeros((LATERAL_LINES, 4), jnp.int32).at[line_labels].set(by_position)
    return table.astype(jnp.int32)


def plant(values, stream_key, least, largest):
    extent = values.shape
    index_at = [jax.random.randint(jax.random.fold_in(stream_key, axis), (), 0, extent[axis]) for axis in range(len(extent))]
    values = values.at[tuple(index_at)].set(least)
    longest = extent.index(max(extent))
    index_at[longest] = (index_at[longest] + 1) % extent[longest]
    return values.at[tuple(index_at)].set(largest)


def shard_levels(own_key, dims, cuts, low, top_value):
    gain = 1.0
    for dim, blocks in cuts:
        draws = jax.random.uniform(jax.random.fold_in(jax.random.fold_in(own_key, 6), dim), (blocks,), jnp.float32, low / len(cuts), top_value / len(cuts))
        gain = gain * jnp.repeat(jnp.exp(draws), dims[dim] // blocks).reshape((-1,) + (1,) * (len(dims) - 1 - dim))
    return gain


def normal_values(key, extent, scale, limit, shards=(), kind=jnp.bfloat16):
    level = shard_levels(key, extent, shards, -0.22, 0.18) if shards else 1.0
    drawn = jax.random.normal(key, extent, jnp.float32) * scale * level
    return jnp.minimum(jnp.maximum(drawn, -limit), limit).astype(kind)


def setup_inputs(seed: int = 0) -> dict:
    splits = jax.random.split(jax.random.key(seed), 10)
    densities = normal_values(splits[0], (LATERAL_LINES, DEPTH_CELLS, SPECIES), 1.0, 6.0, ((0, 4), (1, 8)), jnp.float32)
    source = normal_values(splits[1], (LATERAL_LINES, DEPTH_CELLS, SPECIES), 1.0, 6.0, ((0, 4), (1, 8)), jnp.float32)
    jacobian = normal_values(splits[2], (LATERAL_LINES, DEPTH_CELLS, SPECIES * SPECIES), SPECIES ** -0.5, 0.75, ((0, 4), (1, 8)), jnp.float32)
    pattern = plant((jax.random.randint(splits[3], (NTILE, NTILE), 0, 2) < 1).astype(jnp.int32), jax.random.fold_in(splits[3], 1), 0, 1)
    transport = jnp.clip(jnp.exp(math.log(1.0) - 1.609438 * jax.random.uniform(splits[4], (LATERAL_LINES, DEPTH_CELLS, SPECIES), jnp.float32) ** shard_levels(splits[4], (LATERAL_LINES, DEPTH_CELLS, SPECIES), ((0, 4), (1, 8)), -0.2, 0.2)), 0.2, 1.0)
    lateral = jnp.clip(jnp.exp(math.log(1.0) - 2.3025851 * jax.random.uniform(splits[5], (LATERAL_LINES, DEPTH_CELLS, SPECIES), jnp.float32) ** shard_levels(splits[5], (LATERAL_LINES, DEPTH_CELLS, SPECIES), ((0, 4), (1, 8)), -0.2, 0.2)), 0.1, 1.0)
    neighbours = draw_neighbours(jax.random.fold_in(splits[9], 71), 0)
    factor = draw_factor(jax.random.fold_in(splits[9], 71), 0)
    coupling = draw_coupling(jax.random.fold_in(splits[9], 71), 0)
    return {"densities": densities, "source": source, "jacobian": jacobian, "pattern": pattern, "transport": transport, "lateral": lateral, "neighbours": neighbours, "factor": factor, "coupling": coupling}


def reference(densities, source, jacobian, pattern, transport, lateral, neighbours, factor, coupling):
    highest = lax.Precision.HIGHEST
    mask = jnp.repeat(jnp.repeat(pattern, TILE, axis=0), TILE, axis=1).astype(jnp.float32)
    neighbour_sum = jnp.sum(densities[neighbours], axis=1)

    def one_line(line_items):
        line_dens, line_source, line_jac, line_trans, line_lat, line_nsum, line_factor, line_coup = line_items
        blocks = line_jac.reshape(DEPTH_CELLS, SPECIES, SPECIES) * mask
        reaction = jnp.einsum("kij,kj->ki", blocks, line_dens, precision=highest)
        flux = line_trans * line_dens
        zero_row = jnp.zeros((1, SPECIES), jnp.float32)
        lower_flux = jnp.concatenate([zero_row, flux[:-1]], axis=0)
        upper_cells = jnp.concatenate([line_dens[1:], zero_row], axis=0)
        operator = reaction - lower_flux - line_trans * upper_cells + line_lat * (4.0 * line_dens - line_nsum)
        residual = line_source - operator
        inverse = line_factor.reshape(DEPTH_CELLS, SPECIES, SPECIES)

        def forward(passed, inputs):
            matrix, rhs_vals, coup_vals = inputs
            value = jnp.dot(matrix, rhs_vals + passed, precision=highest)
            return coup_vals * value, value

        start = jnp.zeros((SPECIES,), jnp.float32)
        unused, forward_vals = lax.scan(forward, start, (inverse, residual, line_coup))

        def backward(after, inputs):
            matrix, fwd_vals, coup_vals = inputs
            value = fwd_vals + jnp.dot(matrix, coup_vals * after, precision=highest)
            return value, value

        unused_two, correction = lax.scan(backward, start, (inverse, forward_vals, line_coup), reverse=True)
        return correction

    return lax.map(one_line, (densities, source, jacobian, transport, lateral, neighbour_sum, factor, coupling))
```

```python
import functools

import jax
import jax.numpy as jnp
from jax import lax
from jax.experimental import pallas as pl
from jax.experimental.pallas import tpu as pltpu
from jax.sharding import PartitionSpec as P

MESH = pl.DeviceIdType.MESH
F32 = jnp.float32
BF16 = jnp.bfloat16
ROWS = 8


def split(x):
    high = x.astype(BF16)
    return high, (x - high.astype(F32)).astype(BF16)


def part(pair, index):
    return pair[0][index], pair[1][index]


def dot3(a, b, dims):
    def one(x, y):
        return lax.dot_general(x, y, dims, preferred_element_type=F32)

    return one(a[0], b[0]) + (one(a[0], b[1]) + one(a[1], b[0]))


def widen(x):
    return jnp.concatenate([x, jnp.zeros_like(x)], axis=x.ndim - 1)


def mats(a, b):
    return dot3(tuple(x[:, :, : x.shape[1]] for x in a), b, (((2,), (1,)), ((0,), (0,))))


def vecs(a, v):
    return dot3(split(widen(v)), a, (((2,), (2,)), ((0,), (0,))))


def row_times(v, a):
    return dot3(split(widen(v)), a, (((1,), (1,)), ((), ())))


def pack(x):
    half = x.shape[0] // 2
    return jnp.concatenate([x[:half], x[half:]], axis=1)


def unpack(x):
    half = x.shape[1] // 2
    return jnp.concatenate([x[:, :half], x[:, half:]], axis=0)


def pairs(x):
    y = x.reshape((x.shape[0] // 2, 2) + x.shape[1:])
    return y[:, 0], y[:, 1]


def pair_up(even, odd):
    y = jnp.stack([even, odd], axis=1)
    return y.reshape((2 * even.shape[0],) + even.shape[1:])


def kernel(
    depth_count,
    lat_count,
    dens_ref,
    source_ref,
    jac_hbm,
    pattern_ref,
    transport_ref,
    lateral_ref,
    neighbours_ref,
    factor_hbm,
    coupling_ref,
    out_ref,
    jac_ref,
    factor_ref,
    inv_ref,
    vec_ref,
    lines_ref,
    row_out,
    row_in,
    mat_out,
    fwd_mats,
    bwd_mats,
    vec_out,
    fwd_vecs,
    bwd_vecs,
    load_sem,
    line_send,
    line_recv,
    row_send,
    row_recv,
    mat_send,
    fwd_mat_recv,
    bwd_mat_recv,
    fwd_send,
    fwd_recv,
    bwd_send,
    bwd_recv,
):
    d = lax.axis_index("depth")
    line = lax.axis_index("lat")
    cells, species = dens_ref.shape[1:]
    width = 2 * species
    chunks = species // 2
    last = depth_count - 1

    load_factor = pltpu.make_async_copy(factor_hbm, factor_ref, load_sem.at[0])
    load_jac = pltpu.make_async_copy(jac_hbm, jac_ref, load_sem.at[1])
    load_factor.start()
    load_jac.start()

    barrier = pltpu.get_barrier_semaphore()

    def greet_depth(e, carry):
        @pl.when(e != d)
        def _():
            pl.semaphore_signal(barrier, inc=1, device_id={"depth": e}, device_id_type=MESH)

        return carry

    def greet_lat(e, carry):
        @pl.when(e != line)
        def _():
            pl.semaphore_signal(barrier, inc=1, device_id={"lat": e}, device_id_type=MESH)

        return carry

    lax.fori_loop(0, depth_count, greet_depth, 0)
    lax.fori_loop(0, lat_count, greet_lat, 0)
    dens = dens_ref[0]
    transport = transport_ref[0]
    coupling = coupling_ref[0]
    flux = transport * dens
    row_out[0] = flux[cells - 1 :, :]
    row_out[1] = dens[:1, :]
    lines_ref[line] = dens
    pl.semaphore_wait(barrier, depth_count + lat_count - 2)

    def line_copy(source, target):
        return pltpu.make_async_remote_copy(
            src_ref=dens_ref.at[0],
            dst_ref=lines_ref.at[source],
            send_sem=line_send.at[target],
            recv_sem=line_recv.at[source],
            device_id={"lat": target},
            device_id_type=MESH,
        )

    def row_copy(which, target):
        return pltpu.make_async_remote_copy(
            src_ref=row_out.at[which],
            dst_ref=row_in.at[which],
            send_sem=row_send.at[which],
            recv_sem=row_recv.at[which],
            device_id={"depth": target},
            device_id_type=MESH,
        )

    def mat_copy(which, source, target):
        return pltpu.make_async_remote_copy(
            src_ref=mat_out.at[which],
            dst_ref=(fwd_mats, bwd_mats)[which].at[source],
            send_sem=mat_send.at[target],
            recv_sem=(fwd_mat_recv, bwd_mat_recv)[which].at[source],
            device_id={"depth": target},
            device_id_type=MESH,
        )

    def vec_copy(which, source, target):
        return pltpu.make_async_remote_copy(
            src_ref=vec_out.at[which],
            dst_ref=(fwd_vecs, bwd_vecs)[which].at[source],
            send_sem=(fwd_send, bwd_send)[which].at[target],
            recv_sem=(fwd_recv, bwd_recv)[which].at[source],
            device_id={"depth": target},
            device_id_type=MESH,
        )

    def each_line(act):
        def body(e, carry):
            @pl.when(e != line)
            def _():
                act(e)

            return carry

        lax.fori_loop(0, lat_count, body, 0)

    def each_later(act):
        def body(e, carry):
            act(e)
            return carry

        lax.fori_loop(d + 1, depth_count, body, 0)

    def each_earlier(act):
        def body(i, carry):
            act(d - 1 - i)
            return carry

        lax.fori_loop(0, d, body, 0)

    each_line(lambda e: line_copy(line, e).start())

    @pl.when(d < last)
    def _():
        row_copy(0, d + 1).start()

    @pl.when(d > 0)
    def _():
        row_copy(1, d - 1).start()

    @pl.when(d == 0)
    def _():
        row_in[0] = jnp.zeros((1, species), F32)

    @pl.when(d == last)
    def _():
        row_in[1] = jnp.zeros((1, species), F32)

    used = [0]

    def settle(values):
        at = used[0]
        used[0] += values.shape[0]
        vec_ref[at : used[0]] = values
        return vec_ref[at : used[0]]

    inv_ref[...] = jnp.zeros_like(inv_ref)
    load_factor.wait()
    for first in range(0, cells, 8):
        for p in range(chunks):
            values = factor_ref[0, first : first + 8, p * width : (p + 1) * width]
            start = first * species + 2 * p
            inv_ref[pl.ds(start, 8, stride=species), :species] = values[:, :species]
            inv_ref[pl.ds(start + 1, 8, stride=species), :species] = values[:, species:]
    inverse = inv_ref[...].reshape(cells, species, width)
    coup = widen(coupling).reshape(cells, 1, width)
    coup_before = jnp.concatenate([jnp.ones((1, 1, width), F32), coup[:-1]], axis=0)
    inv = split(inverse)

    fwd_levels = [split(inverse * coup_before)]
    bwd_levels = [split(inverse * coup)]
    group = cells
    while group > 1:
        group //= 2
        fwd_low, fwd_high = zip(*(pairs(x) for x in fwd_levels[-1]))
        bwd_low, bwd_high = zip(*(pairs(x) for x in bwd_levels[-1]))
        fwd = mats(fwd_high, fwd_low)
        bwd = mats(bwd_low, bwd_high)
        if group > 1:
            fwd_levels.append(split(fwd))
            bwd_levels.append(split(bwd))
    last_coup = coupling[cells - 1 :, :]
    last_column = jnp.broadcast_to(last_coup, (species, species)).T
    mat_out[0] = pack(fwd[0][:, :species] * last_column)
    mat_out[1] = pack(bwd[0][:, :species])
    each_later(lambda e: mat_copy(0, d, e).start())
    each_earlier(lambda e: mat_copy(1, d, e).start())

    tiles = pattern_ref.shape[0]
    tile = species // tiles
    lane = lax.broadcasted_iota(jnp.int32, (tiles, width), 1)
    row = lax.broadcasted_iota(jnp.int32, (tiles, width), 0)
    spread = jnp.where((lane % species) // tile == row, 1.0, 0.0).astype(BF16)
    mask_rows = jnp.dot(
        pattern_ref[...].astype(F32).astype(BF16), spread, preferred_element_type=F32
    )
    dens_twice = jnp.concatenate([dens, dens], axis=1)
    at_row = lax.broadcasted_iota(jnp.int32, (width, species), 0) // species
    at_column = lax.broadcasted_iota(jnp.int32, (width, species), 1)
    offset = at_column - at_row
    load_jac.wait()
    reaction = jnp.zeros((cells, species), F32)
    masked = [mask_rows[t : t + 1] * dens_twice for t in range(tiles)]
    for p in range(chunks):
        terms = split(jac_ref[0, :, p * width : (p + 1) * width] * masked[(2 * p) // tile])
        collect = jnp.where(offset == 2 * p, 1.0, 0.0).astype(BF16)
        reaction += jnp.dot(terms[0], collect, preferred_element_type=F32)
        reaction += jnp.dot(terms[1], collect, preferred_element_type=F32)

    @pl.when(d > 0)
    def _():
        row_copy(0, d).wait_recv()

    @pl.when(d < last)
    def _():
        row_copy(1, d).wait_recv()

    each_line(lambda e: line_copy(e, e).wait_recv())
    near = lines_ref[neighbours_ref[0, 0]]
    for j in range(1, neighbours_ref.shape[1]):
        near += lines_ref[neighbours_ref[0, j]]
    cell = lax.broadcasted_iota(jnp.int32, (cells, species), 0)
    lower_flux = jnp.where(cell == 0, row_in[0], pltpu.roll(flux, 1, 0))
    upper = jnp.where(cell == cells - 1, row_in[1], pltpu.roll(dens, cells - 1, 0))
    operator = (
        reaction - lower_flux - transport * upper + lateral_ref[0] * (4.0 * dens - near)
    )
    residual = source_ref[0] - operator
    pivoted = settle(
        vecs(inv, jnp.broadcast_to(residual.reshape(cells, 1, species), (cells, ROWS, species)))
    )

    heads = []
    carried = pivoted
    for level in fwd_levels:
        low, high = pairs(carried)
        later = tuple(pairs(x)[1] for x in level)
        heads.append(low)
        carried = settle(vecs(later, low) + high)
    vec_out[0] = carried[0][:1] * last_coup
    each_later(lambda e: vec_copy(0, d, e).start())

    def forward_step(e, x):
        mat_copy(0, e, e).wait_recv()
        vec_copy(0, e, e).wait_recv()
        return row_times(x, split(widen(unpack(fwd_mats[e])))) + fwd_vecs[e]

    x = lax.fori_loop(0, d, forward_step, jnp.zeros((ROWS, species), F32))

    entering = x.reshape(1, ROWS, species)
    for level, low in zip(fwd_levels[::-1], heads[::-1]):
        earlier = tuple(pairs(m)[0] for m in level)
        entering = settle(pair_up(entering, vecs(earlier, entering) + low))
    forward_vals = settle(vecs(fwd_levels[0], entering) + pivoted)

    tails = []
    carried = forward_vals
    for level in bwd_levels:
        low, high = pairs(carried)
        earlier = tuple(pairs(m)[0] for m in level)
        tails.append(high)
        carried = settle(low + vecs(earlier, high))
    vec_out[1] = carried[0][:1]
    each_earlier(lambda e: vec_copy(1, d, e).start())

    def backward_step(i, y):
        e = last - i
        mat_copy(1, e, e).wait_recv()
        vec_copy(1, e, e).wait_recv()
        return row_times(y, split(widen(unpack(bwd_mats[e])))) + bwd_vecs[e]

    y = lax.fori_loop(0, last - d, backward_step, jnp.zeros((ROWS, species), F32))
    entering = y.reshape(1, ROWS, species)
    for level, high in zip(bwd_levels[::-1], tails[::-1]):
        later = tuple(pairs(m)[1] for m in level)
        entering = settle(pair_up(vecs(later, entering) + high, entering))
    correction = vecs(bwd_levels[0], entering) + forward_vals
    for k in range(cells):
        out_ref[0, k : k + 1, :] = correction[k][:1]

    each_line(lambda e: line_copy(line, e).wait_send())

    @pl.when(d < last)
    def _():
        row_copy(0, d).wait_send()

    @pl.when(d > 0)
    def _():
        row_copy(1, d).wait_send()

    each_later(lambda e: mat_copy(0, d, e).wait_send())
    each_earlier(lambda e: mat_copy(1, d, e).wait_send())
    each_later(lambda e: vec_copy(0, d, e).wait_send())
    each_earlier(lambda e: vec_copy(1, d, e).wait_send())


def on_device(
    densities, source, jacobian, pattern, transport, lateral, neighbours, factor, coupling
):
    lines, cells, species = densities.shape
    depth_count = lax.axis_size("depth")
    lat_count = lax.axis_size("lat")
    vmem = pl.BlockSpec(memory_space=pltpu.VMEM)
    smem = pl.BlockSpec(memory_space=pltpu.SMEM)
    hbm = pl.BlockSpec(memory_space=pl.ANY)
    dma = pltpu.SemaphoreType.DMA
    return pl.pallas_call(
        functools.partial(kernel, depth_count, lat_count),
        out_shape=jax.ShapeDtypeStruct(densities.shape, F32),
        in_specs=[vmem, vmem, hbm, vmem, vmem, vmem, smem, hbm, vmem],
        out_specs=vmem,
        scratch_shapes=[
            pltpu.VMEM(jacobian.shape, F32),
            pltpu.VMEM(factor.shape, F32),
            pltpu.VMEM((cells * species, 2 * species), F32),
            pltpu.VMEM((8 * cells, ROWS, species), F32),
            pltpu.VMEM((lat_count, cells, species), F32),
            pltpu.VMEM((2, 1, species), F32),
            pltpu.VMEM((2, 1, species), F32),
            pltpu.VMEM((2, species // 2, 2 * species), F32),
            pltpu.VMEM((depth_count, species // 2, 2 * species), F32),
            pltpu.VMEM((depth_count, species // 2, 2 * species), F32),
            pltpu.VMEM((2, 1, species), F32),
            pltpu.VMEM((depth_count, 1, species), F32),
            pltpu.VMEM((depth_count, 1, species), F32),
            dma((2,)),
            dma((lat_count,)),
            dma((lat_count,)),
            dma((2,)),
            dma((2,)),
            dma((depth_count,)),
            dma((depth_count,)),
            dma((depth_count,)),
            dma((depth_count,)),
            dma((depth_count,)),
            dma((depth_count,)),
            dma((depth_count,)),
        ],
        compiler_params=pltpu.CompilerParams(
            collective_id=0, has_side_effects=True, vmem_limit_bytes=48 * 1024 * 1024
        ),
    )(densities, source, jacobian, pattern, transport, lateral, neighbours, factor, coupling)


def solution(mesh):
    return jax.shard_map(
        on_device,
        mesh=mesh,
        in_specs=(
            P("lat", "depth", None),
            P("lat", "depth", None),
            P("lat", "depth", None),
            P(),
            P("lat", "depth", None),
            P("lat", "depth", None),
            P("lat", None),
            P("lat", "depth", None),
            P("lat", "depth", None),
        ),
        out_specs=P("lat", "depth", None),
        check_vma=False,
    )
```

```python
import functools

import jax
import jax.numpy as jnp
from jax import lax
from jax.experimental import pallas as pl
from jax.experimental.pallas import tpu as pltpu
from jax.sharding import PartitionSpec as P

MESH = pl.DeviceIdType.MESH
F32 = jnp.float32
BF16 = jnp.bfloat16
ROWS = 8


def split(x):
    high = x.astype(BF16)
    return high, (x - high.astype(F32)).astype(BF16)


def part(pair, index):
    return pair[0][index], pair[1][index]


def dot3(a, b, dims):
    def one(x, y):
        return lax.dot_general(x, y, dims, preferred_element_type=F32)

    return one(a[0], b[0]) + (one(a[0], b[1]) + one(a[1], b[0]))


def widen(x):
    return jnp.concatenate([x, jnp.zeros_like(x)], axis=x.ndim - 1)


def mats(a, b):
    return dot3(tuple(x[:, :, : x.shape[1]] for x in a), b, (((2,), (1,)), ((0,), (0,))))


def dot_rows(v, a, dims):
    rows = v.ndim - 2
    wide = widen(v)
    high = wide.astype(BF16).astype(F32)
    both = jnp.concatenate([high, wide - high], axis=rows).astype(BF16)
    total = lax.dot_general(both, a[0], dims, preferred_element_type=F32)
    total += lax.dot_general(both, a[1], dims, preferred_element_type=F32)
    return total[..., :ROWS, :] + total[..., ROWS:, :]


def vecs(a, v):
    return dot_rows(v, a, (((2,), (2,)), ((0,), (0,))))


def row_times(v, a):
    return dot_rows(v, a, (((1,), (1,)), ((), ())))


def pack(x):
    half = x.shape[0] // 2
    return jnp.concatenate([x[:half], x[half:]], axis=1)


def unpack(x):
    half = x.shape[1] // 2
    return jnp.concatenate([x[:, :half], x[:, half:]], axis=0)


def pairs(x):
    y = x.reshape((x.shape[0] // 2, 2) + x.shape[1:])
    return y[:, 0], y[:, 1]


def pair_up(even, odd):
    y = jnp.stack([even, odd], axis=1)
    return y.reshape((2 * even.shape[0],) + even.shape[1:])


def kernel(
    depth_count,
    lat_count,
    dens_ref,
    source_ref,
    jac_hbm,
    pattern_ref,
    transport_ref,
    lateral_ref,
    neighbours_ref,
    factor_hbm,
    coupling_ref,
    out_ref,
    jac_ref,
    factor_ref,
    inv_ref,
    vec_ref,
    lines_ref,
    row_out,
    row_in,
    mat_out,
    fwd_mats,
    bwd_mats,
    vec_out,
    fwd_vecs,
    bwd_vecs,
    load_sem,
    line_send,
    line_recv,
    row_send,
    row_recv,
    mat_send,
    fwd_mat_recv,
    bwd_mat_recv,
    fwd_send,
    fwd_recv,
    bwd_send,
    bwd_recv,
):
    d = lax.axis_index("depth")
    line = lax.axis_index("lat")
    cells, species = dens_ref.shape[1:]
    width = 2 * species
    chunks = species // 2
    last = depth_count - 1

    load_factor = pltpu.make_async_copy(factor_hbm, factor_ref, load_sem.at[0])
    load_jac = pltpu.make_async_copy(jac_hbm, jac_ref, load_sem.at[1])
    load_factor.start()
    load_jac.start()

    barrier = pltpu.get_barrier_semaphore()

    def greet_depth(e, carry):
        @pl.when(e != d)
        def _():
            pl.semaphore_signal(barrier, inc=1, device_id={"depth": e}, device_id_type=MESH)

        return carry

    def greet_lat(e, carry):
        @pl.when(e != line)
        def _():
            pl.semaphore_signal(barrier, inc=1, device_id={"lat": e}, device_id_type=MESH)

        return carry

    lax.fori_loop(0, depth_count, greet_depth, 0)
    lax.fori_loop(0, lat_count, greet_lat, 0)
    dens = dens_ref[0]
    transport = transport_ref[0]
    coupling = coupling_ref[0]
    flux = transport * dens
    row_out[0] = flux[cells - 1 :, :]
    row_out[1] = dens[:1, :]
    lines_ref[line] = dens
    pl.semaphore_wait(barrier, depth_count + lat_count - 2)

    def line_copy(source, target):
        return pltpu.make_async_remote_copy(
            src_ref=dens_ref.at[0],
            dst_ref=lines_ref.at[source],
            send_sem=line_send.at[target],
            recv_sem=line_recv.at[source],
            device_id={"lat": target},
            device_id_type=MESH,
        )

    def row_copy(which, target):
        return pltpu.make_async_remote_copy(
            src_ref=row_out.at[which],
            dst_ref=row_in.at[which],
            send_sem=row_send.at[which],
            recv_sem=row_recv.at[which],
            device_id={"depth": target},
            device_id_type=MESH,
        )

    def mat_copy(which, source, target):
        return pltpu.make_async_remote_copy(
            src_ref=mat_out.at[which],
            dst_ref=(fwd_mats, bwd_mats)[which].at[source],
            send_sem=mat_send.at[target],
            recv_sem=(fwd_mat_recv, bwd_mat_recv)[which].at[source],
            device_id={"depth": target},
            device_id_type=MESH,
        )

    def vec_copy(which, source, target):
        return pltpu.make_async_remote_copy(
            src_ref=vec_out.at[which],
            dst_ref=(fwd_vecs, bwd_vecs)[which].at[source],
            send_sem=(fwd_send, bwd_send)[which].at[target],
            recv_sem=(fwd_recv, bwd_recv)[which].at[source],
            device_id={"depth": target},
            device_id_type=MESH,
        )

    def each_line(act):
        def body(e, carry):
            @pl.when(e != line)
            def _():
                act(e)

            return carry

        lax.fori_loop(0, lat_count, body, 0)

    def each_later(act):
        def body(e, carry):
            act(e)
            return carry

        lax.fori_loop(d + 1, depth_count, body, 0)

    def each_earlier(act):
        def body(i, carry):
            act(d - 1 - i)
            return carry

        lax.fori_loop(0, d, body, 0)

    each_line(lambda e: line_copy(line, e).start())

    @pl.when(d < last)
    def _():
        row_copy(0, d + 1).start()

    @pl.when(d > 0)
    def _():
        row_copy(1, d - 1).start()

    @pl.when(d == 0)
    def _():
        row_in[0] = jnp.zeros((1, species), F32)

    @pl.when(d == last)
    def _():
        row_in[1] = jnp.zeros((1, species), F32)

    used = [0]

    def settle(values):
        at = used[0]
        used[0] += values.shape[0]
        vec_ref[at : used[0]] = values
        return vec_ref[at : used[0]]

    inv_ref[...] = jnp.zeros_like(inv_ref)
    load_factor.wait()
    for first in range(0, cells, 8):
        for p in range(chunks):
            values = factor_ref[0, first : first + 8, p * width : (p + 1) * width]
            start = first * species + 2 * p
            inv_ref[pl.ds(start, 8, stride=species), :species] = values[:, :species]
            inv_ref[pl.ds(start + 1, 8, stride=species), :species] = values[:, species:]
    inverse = inv_ref[...].reshape(cells, species, width)
    coup = widen(coupling).reshape(cells, 1, width)
    coup_before = jnp.concatenate([jnp.ones((1, 1, width), F32), coup[:-1]], axis=0)
    inv = split(inverse)

    fwd_levels = [split(inverse * coup_before)]
    bwd_levels = [split(inverse * coup)]
    group = cells
    while group > 1:
        group //= 2
        fwd_low, fwd_high = zip(*(pairs(x) for x in fwd_levels[-1]))
        bwd_low, bwd_high = zip(*(pairs(x) for x in bwd_levels[-1]))
        fwd = mats(fwd_high, fwd_low)
        bwd = mats(bwd_low, bwd_high)
        if group > 1:
            fwd_levels.append(split(fwd))
            bwd_levels.append(split(bwd))
    last_coup = coupling[cells - 1 :, :]
    last_column = jnp.broadcast_to(last_coup, (species, species)).T
    mat_out[0] = pack(fwd[0][:, :species] * last_column)
    mat_out[1] = pack(bwd[0][:, :species])
    each_later(lambda e: mat_copy(0, d, e).start())
    each_earlier(lambda e: mat_copy(1, d, e).start())

    tiles = pattern_ref.shape[0]
    tile = species // tiles
    lane = lax.broadcasted_iota(jnp.int32, (tiles, width), 1)
    row = lax.broadcasted_iota(jnp.int32, (tiles, width), 0)
    spread = jnp.where((lane % species) // tile == row, 1.0, 0.0).astype(BF16)
    mask_rows = jnp.dot(
        pattern_ref[...].astype(F32).astype(BF16), spread, preferred_element_type=F32
    )
    dens_twice = jnp.concatenate([dens, dens], axis=1)
    at_row = lax.broadcasted_iota(jnp.int32, (width, species), 0) // species
    at_column = lax.broadcasted_iota(jnp.int32, (width, species), 1)
    offset = at_column - at_row
    load_jac.wait()
    reaction = jnp.zeros((cells, species), F32)
    masked = [mask_rows[t : t + 1] * dens_twice for t in range(tiles)]
    for p in range(chunks):
        terms = split(jac_ref[0, :, p * width : (p + 1) * width] * masked[(2 * p) // tile])
        collect = jnp.where(offset == 2 * p, 1.0, 0.0).astype(BF16)
        reaction += jnp.dot(terms[0], collect, preferred_element_type=F32)
        reaction += jnp.dot(terms[1], collect, preferred_element_type=F32)

    @pl.when(d > 0)
    def _():
        row_copy(0, d).wait_recv()

    @pl.when(d < last)
    def _():
        row_copy(1, d).wait_recv()

    each_line(lambda e: line_copy(e, e).wait_recv())
    near = lines_ref[neighbours_ref[0, 0]]
    for j in range(1, neighbours_ref.shape[1]):
        near += lines_ref[neighbours_ref[0, j]]
    cell = lax.broadcasted_iota(jnp.int32, (cells, species), 0)
    lower_flux = jnp.where(cell == 0, row_in[0], pltpu.roll(flux, 1, 0))
    upper = jnp.where(cell == cells - 1, row_in[1], pltpu.roll(dens, cells - 1, 0))
    operator = (
        reaction - lower_flux - transport * upper + lateral_ref[0] * (4.0 * dens - near)
    )
    residual = source_ref[0] - operator
    pivoted = settle(
        vecs(inv, jnp.broadcast_to(residual.reshape(cells, 1, species), (cells, ROWS, species)))
    )

    heads = []
    carried = pivoted
    for level in fwd_levels:
        low, high = pairs(carried)
        later = tuple(pairs(x)[1] for x in level)
        heads.append(low)
        carried = settle(vecs(later, low) + high)
    vec_out[0] = carried[0][:1] * last_coup
    each_later(lambda e: vec_copy(0, d, e).start())

    def forward_step(e, x):
        mat_copy(0, e, e).wait_recv()
        vec_copy(0, e, e).wait_recv()
        return row_times(x, split(widen(unpack(fwd_mats[e])))) + fwd_vecs[e]

    x = lax.fori_loop(0, d, forward_step, jnp.zeros((ROWS, species), F32))

    entering = x.reshape(1, ROWS, species)
    for level, low in zip(fwd_levels[::-1], heads[::-1]):
        earlier = tuple(pairs(m)[0] for m in level)
        entering = settle(pair_up(entering, vecs(earlier, entering) + low))
    forward_vals = settle(vecs(fwd_levels[0], entering) + pivoted)

    tails = []
    carried = forward_vals
    for level in bwd_levels:
        low, high = pairs(carried)
        earlier = tuple(pairs(m)[0] for m in level)
        tails.append(high)
        carried = settle(low + vecs(earlier, high))
    vec_out[1] = carried[0][:1]
    each_earlier(lambda e: vec_copy(1, d, e).start())

    def backward_step(i, y):
        e = last - i
        mat_copy(1, e, e).wait_recv()
        vec_copy(1, e, e).wait_recv()
        return row_times(y, split(widen(unpack(bwd_mats[e])))) + bwd_vecs[e]

    y = lax.fori_loop(0, last - d, backward_step, jnp.zeros((ROWS, species), F32))
    entering = y.reshape(1, ROWS, species)
    for level, high in zip(bwd_levels[::-1], tails[::-1]):
        later = tuple(pairs(m)[1] for m in level)
        entering = settle(pair_up(vecs(later, entering) + high, entering))
    correction = vecs(bwd_levels[0], entering) + forward_vals
    for k in range(cells):
        out_ref[0, k : k + 1, :] = correction[k][:1]

    each_line(lambda e: line_copy(line, e).wait_send())

    @pl.when(d < last)
    def _():
        row_copy(0, d).wait_send()

    @pl.when(d > 0)
    def _():
        row_copy(1, d).wait_send()

    each_later(lambda e: mat_copy(0, d, e).wait_send())
    each_earlier(lambda e: mat_copy(1, d, e).wait_send())
    each_later(lambda e: vec_copy(0, d, e).wait_send())
    each_earlier(lambda e: vec_copy(1, d, e).wait_send())


def on_device(
    densities, source, jacobian, pattern, transport, lateral, neighbours, factor, coupling
):
    lines, cells, species = densities.shape
    depth_count = lax.axis_size("depth")
    lat_count = lax.axis_size("lat")
    vmem = pl.BlockSpec(memory_space=pltpu.VMEM)
    smem = pl.BlockSpec(memory_space=pltpu.SMEM)
    hbm = pl.BlockSpec(memory_space=pl.ANY)
    dma = pltpu.SemaphoreType.DMA
    return pl.pallas_call(
        functools.partial(kernel, depth_count, lat_count),
        out_shape=jax.ShapeDtypeStruct(densities.shape, F32),
        in_specs=[vmem, vmem, hbm, vmem, vmem, vmem, smem, hbm, vmem],
        out_specs=vmem,
        scratch_shapes=[
            pltpu.VMEM(jacobian.shape, F32),
            pltpu.VMEM(factor.shape, F32),
            pltpu.VMEM((cells * species, 2 * species), F32),
            pltpu.VMEM((8 * cells, ROWS, species), F32),
            pltpu.VMEM((lat_count, cells, species), F32),
            pltpu.VMEM((2, 1, species), F32),
            pltpu.VMEM((2, 1, species), F32),
            pltpu.VMEM((2, species // 2, 2 * species), F32),
            pltpu.VMEM((depth_count, species // 2, 2 * species), F32),
            pltpu.VMEM((depth_count, species // 2, 2 * species), F32),
            pltpu.VMEM((2, 1, species), F32),
            pltpu.VMEM((depth_count, 1, species), F32),
            pltpu.VMEM((depth_count, 1, species), F32),
            dma((2,)),
            dma((lat_count,)),
            dma((lat_count,)),
            dma((2,)),
            dma((2,)),
            dma((depth_count,)),
            dma((depth_count,)),
            dma((depth_count,)),
            dma((depth_count,)),
            dma((depth_count,)),
            dma((depth_count,)),
            dma((depth_count,)),
        ],
        compiler_params=pltpu.CompilerParams(
            collective_id=0, has_side_effects=True, vmem_limit_bytes=48 * 1024 * 1024
        ),
    )(densities, source, jacobian, pattern, transport, lateral, neighbours, factor, coupling)


def solution(mesh):
    return jax.shard_map(
        on_device,
        mesh=mesh,
        in_specs=(
            P("lat", "depth", None),
            P("lat", "depth", None),
            P("lat", "depth", None),
            P(),
            P("lat", "depth", None),
            P("lat", "depth", None),
            P("lat", None),
            P("lat", "depth", None),
            P("lat", "depth", None),
        ),
        out_specs=P("lat", "depth", None),
        check_vma=False,
    )
```
